256 devices in a mesh: seq: 32 (over z, x_hi, core), resp: 8 (over x_lo, y).
Axes of the slice: x: 4 (x_hi: 2, x_lo: 2; x = x_hi * 2 + x_lo), y: 4, z: 8, core: 2. Of those that a mesh axis runs over, the one named last changes fastest.
Arguments:
- queries: bfloat16 [8, 32, 128, 128], P('resp', 'seq'), may hold values from -6 to 6
- grad_out: bfloat16 [8, 32, 128, 128], P('resp', 'seq'), may hold values from -6 to 6
- outputs: bfloat16 [8, 32, 128, 128], P('resp', 'seq'), may hold values from -6 to 6
- log_sums: float32 [8, 32, 128], P('resp', 'seq'), may hold values from 3 to 5
- prompt_keys: bfloat16 [32768, 8, 128], P('seq'), may hold values from -6 to 6
- prompt_values: bfloat16 [32768, 8, 128], P('seq'), may hold values from -6 to 6
Outputs:
- grad_queries: bfloat16 [8, 32, 128, 128], P('resp', 'seq')
- grad_keys: bfloat16 [32768, 8, 128], P('seq', 'resp')
- grad_values: bfloat16 [32768, 8, 128], P('seq', 'resp')
The draws below stay inside these ranges and needn't reach their ends.
All inputs are finite; a program needn't handle non-finite values.
Results may differ from the reference program's by a relative error of at most 0.03.
Values may be sent and summed in bfloat16 or wider, within the bound.
A program may use at most 64 MiB of HBM per device.

```python
import jax
import jax.numpy as jnp
from jax import lax

HEADS = 32
KV_HEADS = 8
HEAD_DIM = 128
RESP_LEN = 128
RESPONSES = 8
PROMPT = 32768


def steps_of(own_key, shape, shards, least, top_value):
    def one(axis_at, parts):
        draws = jax.random.uniform(jax.random.fold_in(jax.random.fold_in(own_key, 6), axis_at), (parts,), jnp.float32, least / len(shards), top_value / len(shards))
        return jnp.repeat(jnp.exp(draws), shape[axis_at] // parts).reshape((-1,) + (1,) * (len(shape) - axis_at - 1))

    factor_of = one(*shards[0])
    for cut in shards[1:]:
        factor_of = factor_of * one(*cut)
    return factor_of


def scatter_about(key, extent, width, most, pieces=(), held_as=jnp.bfloat16):
    array = jax.random.normal(key, extent, jnp.float32) * width
    if len(pieces) > 0:
        array = steps_of(key, extent, pieces, -0.22, 0.18) * array
    return jnp.clip(array, min=-most, max=most).astype(held_as)


def setup_inputs(seed: int = 0) -> dict:
    arg_keys = jax.random.split(jax.random.key(seed), 7)
    queries = scatter_about(arg_keys[0], (RESPONSES, HEADS, RESP_LEN, HEAD_DIM), 1.0, 6.0, ((0, 8), (1, 32)))
    grad_out = scatter_about(arg_keys[1], (RESPONSES, HEADS, RESP_LEN, HEAD_DIM), 1.0, 6.0, ((0, 8), (1, 32)))
    outputs = scatter_about(arg_keys[2], (RESPONSES, HEADS, RESP_LEN, HEAD_DIM), 1.0, 6.0, ((0, 8), (1, 32)))
    log_sums = jnp.clip(3.0 + 2.0 * jax.random.uniform(arg_keys[3], (RESPONSES, HEADS, RESP_LEN), jnp.float32) ** steps_of(arg_keys[3], (RESPONSES, HEADS, RESP_LEN), ((0, 8), (1, 32)), -0.2, 0.2), 3.0, 5.0)
    prompt_keys = scatter_about(arg_keys[4], (PROMPT, KV_HEADS, HEAD_DIM), 1.0, 6.0, ((0, 32),))
    prompt_values = scatter_about(arg_keys[5], (PROMPT, KV_HEADS, HEAD_DIM), 1.0, 6.0, ((0, 32),))
    return {"queries": queries, "grad_out": grad_out, "outputs": outputs, "log_sums": log_sums, "prompt_keys": prompt_keys, "prompt_values": prompt_values}


def rounded(array_in):
    return lax.optimization_barrier(array_in.astype(jnp.bfloat16)).astype(jnp.float32)


def group_terms(query, grad_resp, delta_rows, sums_rows, head_keys, head_values):
    scale_factor = query.shape[-1] ** -0.5
    query_full = query.astype(jnp.float32)
    grad_full = grad_resp.astype(jnp.float32)
    keys_full = head_keys.astype(jnp.float32)
    values_full = head_values.astype(jnp.float32)
    scores = jnp.einsum("gld,pd->glp", query_full, keys_full) * scale_factor
    weights = jnp.exp(scores - sums_rows[:, :, None])
    grad_probs = jnp.einsum("gld,pd->glp", grad_full, values_full)
    grad_scores = rounded(weights * (grad_probs - delta_rows[:, :, None]) * scale_factor)
    grad_query = jnp.einsum("glp,pd->gld", grad_scores, keys_full)
    grad_key = jnp.einsum("glp,gld->pd", grad_scores, query_full)
    grad_value = jnp.einsum("glp,gld->pd", rounded(weights), grad_full)
    return grad_query, grad_key, grad_value


def reference(queries, grad_out, outputs, log_sums, prompt_keys, prompt_values):
    heads_total = queries.shape[1]
    kv_total = prompt_keys.shape[1]
    per_group = heads_total // kv_total
    row_delta = jnp.sum(grad_out.astype(jnp.float32) * outputs.astype(jnp.float32), axis=-1)
    keys_by_head = jnp.transpose(prompt_keys, (1, 0, 2))
    values_by_head = jnp.transpose(prompt_values, (1, 0, 2))

    def shaped(array_in):
        return array_in.reshape((kv_total, per_group) + array_in.shape[1:])

    def per_kv(items):
        return group_terms(items[0], items[1], items[2], items[3], items[4], items[5])

    def per_response(totals, inputs):
        query_resp, grad_resp, delta_resp, sums_resp = inputs
        grad_query, grad_key, grad_value = lax.map(per_kv, (shaped(query_resp), shaped(grad_resp), shaped(delta_resp), shaped(sums_resp), keys_by_head, values_by_head))
        return (totals[0] + rounded(grad_key), totals[1] + rounded(grad_value)), grad_query.reshape(query_resp.shape)

    zeros_kv = jnp.zeros(keys_by_head.shape, jnp.float32)
    (sum_key, sum_value), grad_query = lax.scan(per_response, (zeros_kv, zeros_kv), (queries, grad_out, row_delta, log_sums))
    grad_keys = jnp.transpose(sum_key, (1, 0, 2)).astype(jnp.bfloat16)
    grad_values = jnp.transpose(sum_value, (1, 0, 2)).astype(jnp.bfloat16)
    return grad_query.astype(jnp.bfloat16), grad_keys, grad_values
```

```python
import jax
import jax.numpy as jnp
from jax import lax
from jax.experimental import pallas as pl
from jax.experimental.pallas import tpu as pltpu
from jax.sharding import PartitionSpec as P

NT = (((1,), (1,)), ((), ()))
NN = (((1,), (0,)), ((), ()))
LOG2E = 1.4426950408889634
CHUNK = 4
STEP = 512


def group_kernel(rows_ref, stats_ref, keys_ref, values_ref, dq_ref, dk_ref, dv_ref, keys_t, acc_k, acc_v):
    blocks, _, rows, dim = rows_ref.shape
    positions = keys_ref.shape[0]
    scale = dim**-0.5
    keys_t[...] = keys_ref[...].T
    acc_k[...] = jnp.zeros_like(acc_k)
    acc_v[...] = jnp.zeros_like(acc_v)

    @pl.loop(0, blocks // CHUNK)
    def _(step):
        first = step * CHUNK
        query = jnp.concatenate([rows_ref[first + j, 0] for j in range(CHUNK)], axis=0)
        grad = jnp.concatenate([rows_ref[first + j, 1] for j in range(CHUNK)], axis=0)
        sums = jnp.concatenate([stats_ref[first + j, 0:1, :] for j in range(CHUNK)], axis=1) * LOG2E
        delta = jnp.concatenate([stats_ref[first + j, 1:2, :] for j in range(CHUNK)], axis=1)
        total = None
        for at in range(0, positions, STEP):
            part = pl.ds(at, STEP)
            keys = keys_ref[part, :]
            scores = lax.dot_general(keys, query, NT, preferred_element_type=jnp.float32)
            probs = lax.dot_general(values_ref[part, :], grad, NT, preferred_element_type=jnp.float32)
            weights = jnp.exp2(scores * (scale * LOG2E) - sums)
            low = weights.astype(jnp.bfloat16)
            grad_scores = (weights * (probs - delta)).astype(jnp.bfloat16)
            acc_v[part, :] += lax.dot_general(low, grad, NN, preferred_element_type=jnp.float32)
            acc_k[part, :] += lax.dot_general(grad_scores, query, NN, preferred_element_type=jnp.float32)
            term = lax.dot_general(keys_t[:, part], grad_scores, NN, preferred_element_type=jnp.float32)
            total = term if total is None else total + term
        total = (total * scale).astype(jnp.bfloat16)
        for j in range(CHUNK):
            dq_ref[first + j] = total[:, j * rows : (j + 1) * rows]

    dk_ref[...] = (acc_k[...] * scale).astype(dk_ref.dtype)
    dv_ref[...] = acc_v[...].astype(dv_ref.dtype)


def grouped(rows, stats, keys, values):
    vmem = pl.BlockSpec(memory_space=pltpu.VMEM)
    blocks, _, length, dim = rows.shape
    positions = keys.shape[0]
    return pl.pallas_call(
        group_kernel,
        out_shape=(
            jax.ShapeDtypeStruct((blocks, dim, length), jnp.bfloat16),
            jax.ShapeDtypeStruct((positions, dim), jnp.bfloat16),
            jax.ShapeDtypeStruct((positions, dim), jnp.bfloat16),
        ),
        in_specs=[vmem] * 4,
        out_specs=(vmem,) * 3,
        scratch_shapes=[
            pltpu.VMEM((dim, positions), jnp.bfloat16),
            pltpu.VMEM((positions, dim), jnp.float32),
            pltpu.VMEM((positions, dim), jnp.float32),
        ],
        compiler_params=pltpu.CompilerParams(vmem_limit_bytes=40 << 20),
    )(rows, stats, keys, values)


def per_device(queries, grad_out, outputs, log_sums, prompt_keys, prompt_values):
    both = ("seq", "resp")
    there = [
        ((4 * g + j) * 8 + r, (4 * r + j) * 8 + g) for g in range(8) for j in range(4) for r in range(8)
    ]
    back = [(b, a) for a, b in there]
    group = lax.axis_index("resp")
    delta = jnp.sum(grad_out.astype(jnp.float32) * outputs.astype(jnp.float32), axis=-1)
    stats = jnp.stack([log_sums[0, 0], delta[0, 0]])
    rows = jnp.stack([queries[0, 0], grad_out[0, 0]])
    rows = lax.all_gather(lax.ppermute(rows, both, there), "seq", axis=0, tiled=False)
    stats = lax.all_gather(lax.ppermute(stats, both, there), "seq", axis=0, tiled=False)
    keys = lax.dynamic_index_in_dim(prompt_keys, group, 1, keepdims=False)
    values = lax.dynamic_index_in_dim(prompt_values, group, 1, keepdims=False)
    dq, dk, dv = grouped(rows, stats, keys, values)
    own = lax.psum_scatter(dq, "seq", scatter_dimension=0, tiled=True)
    own = lax.ppermute(own, both, back)
    return jnp.swapaxes(own, 1, 2)[None], dk[:, None, :], dv[:, None, :]


def solution(mesh):
    in_specs = (
        P("resp", "seq", None, None),
        P("resp", "seq", None, None),
        P("resp", "seq", None, None),
        P("resp", "seq", None),
        P("seq", None, None),
        P("seq", None, None),
    )
    out_specs = (P("resp", "seq", None, None), P("seq", "resp", None), P("seq", "resp", None))
    return jax.shard_map(
        per_device, mesh=mesh, in_specs=in_specs, out_specs=out_specs, check_vma=False
    )
```

```python
import functools

import jax
import jax.numpy as jnp
from jax import lax
from jax.experimental import pallas as pl
from jax.experimental.pallas import tpu as pltpu
from jax.sharding import PartitionSpec as P

NT = (((1,), (1,)), ((), ()))
NN = (((1,), (0,)), ((), ()))
MESH = pl.DeviceIdType.MESH
LOG2E = 1.4426950408889634
STEP = 512
PLANES = 8
OFFSETS = (0, 7, 1, 6, 2, 5, 3, 4)


def split3(row):
    high = row.astype(jnp.bfloat16).astype(jnp.float32)
    rest = row - high
    mid = rest.astype(jnp.bfloat16).astype(jnp.float32)
    return [high, mid, rest - mid]


def kernel(
    q_ref, g_ref, o_ref, sums_ref, k_hbm, v_hbm,
    dq_ref, dk_ref, dv_ref,
    pack, blk, part, in1, mid, in2, k_all, v_all, keys, values, keys_t, acc_k, acc_v,
    kv_sem, pre_send, pre_recv, up_send, down_send, ring_recv, sib_send, sib_recv,
    one_send, one_recv, two_send, two_recv,
):
    seq, grp = lax.axis_index("seq"), lax.axis_index("resp")
    z, j = seq // 4, lax.rem(seq, 4)
    xh, core = j // 2, lax.rem(j, 2)
    rows = q_ref.shape[0]
    positions = dk_ref.shape[0]
    groups = k_all.shape[0] // positions
    scale = q_ref.shape[1] ** -0.5

    def wrap(value):
        return lax.rem(value + 2 * PLANES, PLANES)

    def remote(src, dst, send, recv, seq_to, resp_to):
        return pltpu.make_async_remote_copy(
            src_ref=src, dst_ref=dst, send_sem=send, recv_sem=recv,
            device_id=(seq_to, resp_to), device_id_type=MESH,
        )

    def arrived(ref, sem):
        pltpu.make_async_copy(ref, ref, sem).wait()

    load_k = pltpu.make_async_copy(k_hbm, k_all, kv_sem.at[0])
    load_v = pltpu.make_async_copy(v_hbm, v_all, kv_sem.at[1])
    load_k.start()
    load_v.start()

    barrier = pltpu.get_barrier_semaphore()
    source = wrap(z - grp)
    pre_seq = wrap(grp + z) * 4 + core
    on_self = jnp.logical_and(grp == 0, z == 0)

    @pl.loop(1, 4 * PLANES)
    def _(t):
        other = lax.rem(grp * 4 + j + t, 4 * PLANES)
        pl.semaphore_signal(
            barrier, inc=1, device_id=(z * 4 + lax.rem(other, 4), other // 4), device_id_type=MESH
        )

    @pl.loop(1, PLANES)
    def _(t):
        pl.semaphore_signal(
            barrier, inc=1, device_id=(lax.rem(z + t, PLANES) * 4 + j, grp), device_id_type=MESH
        )

    for side in range(2):
        here = jnp.logical_and(on_self, xh == side)

        @pl.when(jnp.logical_not(here))
        def _():
            pl.semaphore_signal(
                barrier, inc=1, device_id=(grp * 4 + 2 * side + core, source), device_id_type=MESH
            )

    grad_own = g_ref[...]
    product = grad_own.astype(jnp.float32) * o_ref[...].astype(jnp.float32)
    delta = jnp.sum(product.T, axis=0, keepdims=True)
    stats = split3(sums_ref[...] * LOG2E) + split3(delta)
    stats = jnp.concatenate(stats + [jnp.zeros((10, rows), jnp.float32)], axis=0)
    pack[0:rows, :] = q_ref[...]
    pack[rows : 2 * rows, :] = grad_own
    pack[2 * rows :, :] = stats.astype(jnp.bfloat16)

    pl.semaphore_wait(barrier, 4 * PLANES - 1 + PLANES - 1 + 2 - on_self.astype(jnp.int32))

    def first(side):
        return remote(
            pack, blk.at[0, core, xh], pre_send.at[side], pre_recv.at[xh], pre_seq + 2 * side, z
        )

    for side in range(2):
        here = jnp.logical_and(on_self, xh == side)

        @pl.when(here)
        def _():
            pltpu.make_async_copy(pack, blk.at[0, core, xh], pre_recv.at[xh]).start()

        @pl.when(jnp.logical_not(here))
        def _():
            first(side).start()

    load_k.wait()
    load_v.wait()
    tile = 128
    pick = (
        lax.broadcasted_iota(jnp.int32, (tile, tile * groups), 1)
        == lax.broadcasted_iota(jnp.int32, (tile, tile * groups), 0) * groups + grp
    ).astype(jnp.bfloat16)
    for t in range(positions // tile):
        wide, narrow = pl.ds(t * tile * groups, tile * groups), pl.ds(t * tile, tile)
        keys[narrow, :] = lax.dot_general(
            pick, k_all[wide, :], NN, preferred_element_type=jnp.float32
        ).astype(jnp.bfloat16)
        values[narrow, :] = lax.dot_general(
            pick, v_all[wide, :], NN, preferred_element_type=jnp.float32
        ).astype(jnp.bfloat16)
    keys_t[...] = keys[...].T
    acc_k[...] = jnp.zeros_like(acc_k)
    acc_v[...] = jnp.zeros_like(acc_v)

    above, below = wrap(z + 1) * 4 + j, wrap(z - 1) * 4 + j
    sibling = z * 4 + 2 * xh + (1 - core)

    def to_sibling(k, s):
        return remote(
            blk.at[k, core, s], blk.at[k, core, s], sib_send.at[k, s], sib_recv.at[k, s], sibling, grp
        )

    def onward(k, s):
        copies = []
        if k == 0:
            steps = ((1, 0), (2, 1))
        elif k in (1, 3):
            steps = ((k + 2, 0),)
        elif k in (2, 4):
            steps = ((k + 2, 1),)
        elif k == 5 and s == 0:
            steps = ((7, 0),)
        elif k == 6 and s == 1:
            steps = ((7, 1),)
        else:
            steps = ()
        for k_to, way in steps:
            copies.append(
                remote(
                    blk.at[k, core, s], blk.at[k_to, core, s],
                    (down_send if way else up_send).at[k, s], ring_recv.at[k_to, s],
                    below if way else above, grp,
                )
            )
        return copies

    def pass_on(k):
        for s in range(2):
            arrived(blk.at[k, core, s], (pre_recv.at[s] if k == 0 else ring_recv.at[k, s]))
            for copy in onward(k, s):
                copy.start()
            to_sibling(k, s).start()

    def work(k):
        parts = [blk.at[k, b // 2, b % 2] for b in range(4)]
        query = jnp.concatenate([p[0:rows, :] for p in parts], axis=0)
        grad = jnp.concatenate([p[rows : 2 * rows, :] for p in parts], axis=0)
        stats = [p[2 * rows :, :].astype(jnp.float32) for p in parts]
        sums = jnp.concatenate([s[0:1] + s[1:2] + s[2:3] for s in stats], axis=1)
        delta = jnp.concatenate([s[3:4] + s[4:5] + s[5:6] for s in stats], axis=1)
        total = None
        for at in range(0, positions, STEP):
            span = pl.ds(at, STEP)
            scores = lax.dot_general(keys[span, :], query, NT, preferred_element_type=jnp.float32)
            probs = lax.dot_general(values[span, :], grad, NT, preferred_element_type=jnp.float32)
            weights = jnp.exp2(scores * (scale * LOG2E) - sums)
            low = weights.astype(jnp.bfloat16)
            grad_scores = (weights * (probs - delta)).astype(jnp.bfloat16)
            acc_v[span, :] += lax.dot_general(low, grad, NN, preferred_element_type=jnp.float32)
            acc_k[span, :] += lax.dot_general(grad_scores, query, NN, preferred_element_type=jnp.float32)
            term = lax.dot_general(keys_t[:, span], grad_scores, NN, preferred_element_type=jnp.float32)
            total = term if total is None else total + term
        total = total.astype(jnp.bfloat16)
        for b in range(4):
            part[k, b] = total[:, b * rows : (b + 1) * rows]

    def spread(k, b):
        owner = (b % 2) * 2 + b // 2
        resp_to = wrap(z + OFFSETS[k] - grp)
        here = jnp.logical_and(owner == j, resp_to == grp)
        copy = remote(
            part.at[k, b], in1.at[k, j], one_send.at[k, b], one_recv.at[k, j], z * 4 + owner, resp_to
        )
        return here, copy

    def send_parts(k):
        for b in range(4):
            here, copy = spread(k, b)

            @pl.when(here)
            def _():
                pltpu.make_async_copy(part.at[k, b], in1.at[k, j], one_recv.at[k, j]).start()

            @pl.when(jnp.logical_not(here))
            def _():
                copy.start()

    def home(k):
        plane = wrap(z + OFFSETS[k] - grp)
        copy = remote(mid.at[k], in2.at[k], two_send.at[k], two_recv.at[k], plane * 4 + j, grp)
        return plane == z, copy

    def combine(k):
        for s in range(4):
            arrived(in1.at[k, s], one_recv.at[k, s])
        total = in1[k, 0].astype(jnp.float32)
        for s in range(1, 4):
            total += in1[k, s].astype(jnp.float32)
        mid[k] = total.astype(jnp.bfloat16)
        here, copy = home(k)

        @pl.when(here)
        def _():
            pltpu.make_async_copy(mid.at[k], in2.at[k], two_recv.at[k]).start()

        @pl.when(jnp.logical_not(here))
        def _():
            copy.start()

    for k in range(PLANES):
        if k in (0, 7):
            pass_on(k)
        elif k % 2 == 1:
            pass_on(k)
            pass_on(k + 1)
        for s in range(2):
            arrived(blk.at[k, 1 - core, s], sib_recv.at[k, s])
        work(k)
        send_parts(k)
        if k >= 2:
            combine(k - 2)
    dk_ref[...] = (acc_k[...] * scale).astype(dk_ref.dtype)
    dv_ref[...] = acc_v[...].astype(dv_ref.dtype)
    combine(PLANES - 2)
    combine(PLANES - 1)

    for k in range(PLANES):
        arrived(in2.at[k], two_recv.at[k])
    total = in2[0].astype(jnp.float32)
    for k in range(1, PLANES):
        total += in2[k].astype(jnp.float32)
    dq_ref[...] = (total * scale).T.astype(dq_ref.dtype)

    for side in range(2):
        here = jnp.logical_and(on_self, xh == side)

        @pl.when(jnp.logical_not(here))
        def _():
            first(side).wait_send()

    for k in range(PLANES):
        for s in range(2):
            for copy in onward(k, s):
                copy.wait_send()
            to_sibling(k, s).wait_send()
        for b in range(4):
            here, copy = spread(k, b)
            pl.when(jnp.logical_not(here))(copy.wait_send)
        here, copy = home(k)
        pl.when(jnp.logical_not(here))(copy.wait_send)


def per_device(queries, grad_out, outputs, log_sums, prompt_keys, prompt_values):
    rows, dim = queries.shape[2:]
    positions, groups = prompt_keys.shape[:2]
    vmem = pl.BlockSpec(memory_space=pltpu.VMEM)
    hbm = pl.BlockSpec(memory_space=pl.ANY)
    dma = pltpu.SemaphoreType.DMA
    low, full = jnp.bfloat16, jnp.float32
    dq, dk, dv = pl.pallas_call(
        kernel,
        out_shape=(
            jax.ShapeDtypeStruct((rows, dim), low),
            jax.ShapeDtypeStruct((positions, dim), low),
            jax.ShapeDtypeStruct((positions, dim), low),
        ),
        in_specs=[vmem] * 4 + [hbm] * 2,
        out_specs=(vmem,) * 3,
        scratch_shapes=[
            pltpu.VMEM((2 * rows + 16, dim), low),
            pltpu.VMEM((PLANES, 2, 2, 2 * rows + 16, dim), low),
            pltpu.VMEM((PLANES, 4, dim, rows), low),
            pltpu.VMEM((PLANES, 4, dim, rows), low),
            pltpu.VMEM((PLANES, dim, rows), low),
            pltpu.VMEM((PLANES, dim, rows), low),
            pltpu.VMEM((positions * groups, dim), low),
            pltpu.VMEM((positions * groups, dim), low),
            pltpu.VMEM((positions, dim), low),
            pltpu.VMEM((positions, dim), low),
            pltpu.VMEM((dim, positions), low),
            pltpu.VMEM((positions, dim), full),
            pltpu.VMEM((positions, dim), full),
            dma((2,)), dma((2,)), dma((2,)),
            dma((PLANES, 2)), dma((PLANES, 2)), dma((PLANES, 2)),
            dma((PLANES, 2)), dma((PLANES, 2)),
            dma((PLANES, 4)), dma((PLANES, 4)), dma((PLANES,)), dma((PLANES,)),
        ],
        compiler_params=pltpu.CompilerParams(
            collective_id=0, has_side_effects=True, vmem_limit_bytes=60 << 20
        ),
    )(
        queries[0, 0], grad_out[0, 0], outputs[0, 0], log_sums[0],
        prompt_keys.reshape(positions * groups, dim), prompt_values.reshape(positions * groups, dim),
    )
    return dq[None, None], dk[:, None, :], dv[:, None, :]


def solution(mesh):
    in_specs = (
        P("resp", "seq", None, None),
        P("resp", "seq", None, None),
        P("resp", "seq", None, None),
        P("resp", "seq", None),
        P("seq", None, None),
        P("seq", None, None),
    )
    out_specs = (P("resp", "seq", None, None), P("seq", "resp", None), P("seq", "resp", None))
    return jax.shard_map(
        per_device, mesh=mesh, in_specs=in_specs, out_specs=out_specs, check_vma=False
    )
```

```python
import functools

import jax
import jax.numpy as jnp
from jax import lax
from jax.experimental import pallas as pl
from jax.experimental.pallas import tpu as pltpu
from jax.sharding import PartitionSpec as P

NT = (((1,), (1,)), ((), ()))
NN = (((1,), (0,)), ((), ()))
MESH = pl.DeviceIdType.MESH
LOG2E = 1.4426950408889634
STEP = 512
PLANES = 8
AHEAD = 5
WINDOW = 3
LAG = 4


def split3(row):
    high = row.astype(jnp.bfloat16).astype(jnp.float32)
    rest = row - high
    mid = rest.astype(jnp.bfloat16).astype(jnp.float32)
    return [high, mid, rest - mid]


def kernel(
    q_ref, g_ref, o_ref, sums_ref, k_hbm, v_hbm,
    dq_ref, dk_ref, dv_ref,
    pack, held, blk, part, other, pair, in1, mid, in2, k_all, v_all, keys, values, keys_t, acc_k, acc_v,
    kv_sem, held_send, held_recv, blk_send, blk_recv, sib_send, sib_recv, core_send, core_recv,
    one_send, one_recv, two_send, two_recv,
):
    seq, grp = lax.axis_index("seq"), lax.axis_index("resp")
    z, j = seq // 4, lax.rem(seq, 4)
    xh, core = j // 2, lax.rem(j, 2)
    rows = q_ref.shape[0]
    positions = dk_ref.shape[0]
    groups = k_all.shape[0] // positions
    scale = q_ref.shape[1] ** -0.5
    sibling = z * 4 + 2 * xh + (1 - core)

    def wrap(value):
        return lax.rem(value + 2 * PLANES, PLANES)

    def remote(src, dst, send, recv, seq_to, resp_to):
        return pltpu.make_async_remote_copy(
            src_ref=src, dst_ref=dst, send_sem=send, recv_sem=recv,
            device_id=(seq_to, resp_to), device_id_type=MESH,
        )

    def arrived(ref, sem):
        pltpu.make_async_copy(ref, ref, sem).wait()

    load_k = pltpu.make_async_copy(k_hbm, k_all, kv_sem.at[0])
    load_v = pltpu.make_async_copy(v_hbm, v_all, kv_sem.at[1])
    load_k.start()
    load_v.start()

    barrier = pltpu.get_barrier_semaphore()

    @pl.loop(1, PLANES)
    def _(t):
        pl.semaphore_signal(
            barrier, inc=1, device_id=(lax.rem(z + t, PLANES) * 4 + j, grp), device_id_type=MESH
        )

    @pl.loop(1, 2 * PLANES)
    def _(t):
        peer = lax.rem(grp * 2 + xh + t, 2 * PLANES)
        pl.semaphore_signal(
            barrier, inc=1, device_id=(z * 4 + 2 * lax.rem(peer, 2) + core, peer // 2),
            device_id_type=MESH,
        )

    pl.semaphore_signal(barrier, inc=1, device_id=(sibling, grp), device_id_type=MESH)

    grad_own = g_ref[...]
    product = grad_own.astype(jnp.float32) * o_ref[...].astype(jnp.float32)
    delta = jnp.sum(product.T, axis=0, keepdims=True)
    stats = split3(sums_ref[...] * LOG2E) + split3(delta)
    stats = jnp.concatenate(stats + [jnp.zeros((10, rows), jnp.float32)], axis=0)
    pack[0:rows, :] = q_ref[...]
    pack[rows : 2 * rows, :] = grad_own
    pack[2 * rows :, :] = stats.astype(jnp.bfloat16)

    pl.semaphore_wait(barrier, PLANES - 1 + 2 * PLANES - 1 + 1)

    def move(here, copy, src, dst, recv):
        pl.when(here)(lambda: pltpu.make_async_copy(src, dst, recv).start())
        pl.when(jnp.logical_not(here))(lambda: copy.start())

    def along(k):
        plane = wrap(z + grp + k)
        return plane == z, remote(
            pack, held.at[k], held_send.at[k], held_recv.at[k], plane * 4 + j, grp
        )

    def launch(k):
        here, copy = along(k)
        move(here, copy, pack, held.at[k], held_recv.at[k])

    for k in range(WINDOW):
        launch(k)

    def across(k, side):
        head = wrap(z - grp - k)
        return jnp.logical_and(head == grp, xh == side), remote(
            held.at[k], blk.at[k, core, xh], blk_send.at[k, side], blk_recv.at[k, xh],
            z * 4 + 2 * side + core, head,
        )

    def forward(k):
        arrived(held.at[k], held_recv.at[k])
        for side in range(2):
            here, copy = across(k, side)
            move(here, copy, held.at[k], blk.at[k, core, xh], blk_recv.at[k, xh])

    def to_sibling(k):
        return remote(blk.at[k, core], blk.at[k, core], sib_send.at[k], sib_recv.at[k], sibling, grp)

    def share(k):
        for s in range(2):
            arrived(blk.at[k, core, s], blk_recv.at[k, s])
        to_sibling(k).start()

    load_k.wait()
    load_v.wait()
    tile = 128
    pick = (
        lax.broadcasted_iota(jnp.int32, (tile, tile * groups), 1)
        == lax.broadcasted_iota(jnp.int32, (tile, tile * groups), 0) * groups + grp
    ).astype(jnp.bfloat16)
    for t in range(positions // tile):
        wide, narrow = pl.ds(t * tile * groups, tile * groups), pl.ds(t * tile, tile)
        keys[narrow, :] = lax.dot_general(
            pick, k_all[wide, :], NN, preferred_element_type=jnp.float32
        ).astype(jnp.bfloat16)
        values[narrow, :] = lax.dot_general(
            pick, v_all[wide, :], NN, preferred_element_type=jnp.float32
        ).astype(jnp.bfloat16)
    keys_t[...] = keys[...].T
    acc_k[...] = jnp.zeros_like(acc_k)
    acc_v[...] = jnp.zeros_like(acc_v)

    def work(k):
        parts = [blk.at[k, b // 2, b % 2] for b in range(4)]
        query = jnp.concatenate([p[0:rows, :] for p in parts], axis=0)
        grad = jnp.concatenate([p[rows : 2 * rows, :] for p in parts], axis=0)
        stats = [p[2 * rows :, :].astype(jnp.float32) for p in parts]
        sums = jnp.concatenate([s[0:1] + s[1:2] + s[2:3] for s in stats], axis=1)
        delta = jnp.concatenate([s[3:4] + s[4:5] + s[5:6] for s in stats], axis=1)
        total = None
        for at in range(0, positions, STEP):
            span = pl.ds(at, STEP)
            scores = lax.dot_general(keys[span, :], query, NT, preferred_element_type=jnp.float32)
            probs = lax.dot_general(values[span, :], grad, NT, preferred_element_type=jnp.float32)
            weights = jnp.exp2(scores * (scale * LOG2E) - sums)
            low = weights.astype(jnp.bfloat16)
            grad_scores = (weights * (probs - delta)).astype(jnp.bfloat16)
            acc_v[span, :] += lax.dot_general(low, grad, NN, preferred_element_type=jnp.float32)
            acc_k[span, :] += lax.dot_general(grad_scores, query, NN, preferred_element_type=jnp.float32)
            term = lax.dot_general(keys_t[:, span], grad_scores, NN, preferred_element_type=jnp.float32)
            total = term if total is None else total + term
        total = total.astype(jnp.bfloat16)
        for b in range(4):
            part[k, b // 2, b % 2] = total[:, b * rows : (b + 1) * rows]

    def to_core(k):
        return remote(
            part.at[k, 1 - core], other.at[k], core_send.at[k], core_recv.at[k], sibling, grp
        )

    def spread(k, s):
        place = wrap(z - grp - k)
        return jnp.logical_and(place == grp, xh == s), remote(
            pair.at[k, s], in1.at[k, xh], one_send.at[k, s], one_recv.at[k, xh],
            z * 4 + 2 * s + core, place,
        )

    def add_cores(k):
        arrived(other.at[k], core_recv.at[k])
        for s in range(2):
            pair[k, s] = (
                part[k, core, s].astype(jnp.float32) + other[k, s].astype(jnp.float32)
            ).astype(jnp.bfloat16)
            here, copy = spread(k, s)
            move(here, copy, pair.at[k, s], in1.at[k, xh], one_recv.at[k, xh])

    def home(k):
        plane = wrap(z - grp - k)
        return plane == z, remote(
            mid.at[k], in2.at[k], two_send.at[k], two_recv.at[k], plane * 4 + j, grp
        )

    def add_plane(k):
        for s in range(2):
            arrived(in1.at[k, s], one_recv.at[k, s])
        mid[k] = (in1[k, 0].astype(jnp.float32) + in1[k, 1].astype(jnp.float32)).astype(jnp.bfloat16)
        here, copy = home(k)
        move(here, copy, mid.at[k], in2.at[k], two_recv.at[k])

    def left(here, copy):
        pl.when(jnp.logical_not(here))(lambda: copy.wait_send())

    for k in range(WINDOW, PLANES):
        left(*along(k - WINDOW))
        launch(k)
        if k >= LAG:
            forward(k - LAG)
    for k in range(PLANES - LAG, AHEAD):
        forward(k)
    share(0)
    for k in range(PLANES):
        if k + AHEAD < PLANES:
            forward(k + AHEAD)
        if k + 1 < PLANES:
            share(k + 1)
        arrived(blk.at[k, 1 - core], sib_recv.at[k])
        work(k)
        to_core(k).start()
        if k >= 1:
            add_cores(k - 1)
        if k >= 4:
            add_plane(k - 4)
    add_cores(PLANES - 1)
    dk_ref[...] = (acc_k[...] * scale).astype(dk_ref.dtype)
    dv_ref[...] = acc_v[...].astype(dv_ref.dtype)
    for k in range(PLANES - 4, PLANES):
        add_plane(k)
    total = jnp.zeros((q_ref.shape[1], rows), jnp.float32)
    for k in range(PLANES):
        arrived(in2.at[k], two_recv.at[k])
        total += in2[k].astype(jnp.float32)
    dq_ref[...] = (total * scale).T.astype(dq_ref.dtype)

    for k in range(PLANES - WINDOW, PLANES):
        left(*along(k))
    for k in range(PLANES):
        for s in range(2):
            left(*across(k, s))
            left(*spread(k, s))
        to_sibling(k).wait_send()
        to_core(k).wait_send()
        left(*home(k))


def copy_kernel(*refs):
    half = len(refs) // 2
    for src, dst in zip(refs[:half], refs[half:]):
        dst[...] = src[...]


def per_device(queries, grad_out, outputs, log_sums, prompt_keys, prompt_values):
    rows, dim = queries.shape[2:]
    positions, groups = prompt_keys.shape[:2]
    vmem = pl.BlockSpec(memory_space=pltpu.VMEM)
    hbm = pl.BlockSpec(memory_space=pl.ANY)
    dma = pltpu.SemaphoreType.DMA
    low, full = jnp.bfloat16, jnp.float32
    dq, dk, dv = pl.pallas_call(
        kernel,
        out_shape=(
            jax.ShapeDtypeStruct((rows, dim), low),
            jax.ShapeDtypeStruct((positions, dim), low),
            jax.ShapeDtypeStruct((positions, dim), low),
        ),
        in_specs=[vmem] * 4 + [hbm] * 2,
        out_specs=(vmem,) * 3,
        scratch_shapes=[
            pltpu.VMEM((2 * rows + 16, dim), low),
            pltpu.VMEM((PLANES, 2 * rows + 16, dim), low),
            pltpu.VMEM((PLANES, 2, 2, 2 * rows + 16, dim), low),
            pltpu.VMEM((PLANES, 2, 2, dim, rows), low),
            pltpu.VMEM((PLANES, 2, dim, rows), low),
            pltpu.VMEM((PLANES, 2, dim, rows), low),
            pltpu.VMEM((PLANES, 2, dim, rows), low),
            pltpu.VMEM((PLANES, dim, rows), low),
            pltpu.VMEM((PLANES, dim, rows), low),
            pltpu.VMEM((positions * groups, dim), low),
            pltpu.VMEM((positions * groups, dim), low),
            pltpu.VMEM((positions, dim), low),
            pltpu.VMEM((positions, dim), low),
            pltpu.VMEM((dim, positions), low),
            pltpu.VMEM((positions, dim), full),
            pltpu.VMEM((positions, dim), full),
            dma((2,)), dma((PLANES,)), dma((PLANES,)),
            dma((PLANES, 2)), dma((PLANES, 2)), dma((PLANES,)), dma((PLANES,)),
            dma((PLANES,)), dma((PLANES,)),
            dma((PLANES, 2)), dma((PLANES, 2)), dma((PLANES,)), dma((PLANES,)),
        ],
        compiler_params=pltpu.CompilerParams(
            collective_id=0, has_side_effects=True, vmem_limit_bytes=60 << 20
        ),
    )(
        queries[0, 0], grad_out[0, 0], outputs[0, 0], log_sums[0],
        prompt_keys.reshape(positions * groups, dim), prompt_values.reshape(positions * groups, dim),
    )
    outs = (dq, dk, dv)
    dq, dk, dv = pl.pallas_call(
        copy_kernel,
        out_shape=tuple(jax.ShapeDtypeStruct(x.shape, x.dtype) for x in outs),
        in_specs=[vmem] * 3,
        out_specs=(vmem,) * 3,
    )(*outs)
    return dq[None, None], dk[:, None, :], dv[:, None, :]


def solution(mesh):
    in_specs = (
        P("resp", "seq", None, None),
        P("resp", "seq", None, None),
        P("resp", "seq", None, None),
        P("resp", "seq", None),
        P("seq", None, None),
        P("seq", None, None),
    )
    out_specs = (P("resp", "seq", None, None), P("seq", "resp", None), P("seq", "resp", None))
    return jax.shard_map(
        per_device, mesh=mesh, in_specs=in_specs, out_specs=out_specs, check_vma=False
    )
```

```python
import functools

import jax
import jax.numpy as jnp
from jax import lax
from jax.experimental import pallas as pl
from jax.experimental.pallas import tpu as pltpu
from jax.sharding import PartitionSpec as P

NT = (((1,), (1,)), ((), ()))
NN = (((1,), (0,)), ((), ()))
MESH = pl.DeviceIdType.MESH
LOG2E = 1.4426950408889634
STEP = 512
PLANES = 8
SPREAD = (4, 3, 6)
ORDER = (2, 5, 0, 4, 7, 3, 1, 6)
AHEAD = 5
WINDOW = 8


def times(columns, value):
    return functools.reduce(lambda x, y: x ^ y, [c for i, c in enumerate(columns) if value >> i & 1], 0)


def inverse(columns):
    return tuple(next(v for v in range(PLANES) if times(columns, v) == 1 << i) for i in range(3))


def mapped(first, a, second, b, constant):
    total = 0
    for i in range(3):
        bit = constant >> i & 1
        for columns, value in ((first, a), (second, b)):
            for n, column in enumerate(columns):
                if column >> i & 1:
                    bit = bit + value[n]
        total = total + lax.rem(bit, 2) * (1 << i)
    return total


def joined(one, two):
    return tuple(x ^ y for x, y in zip(one, two))


SAME = (1, 2, 4)
REST = joined(SPREAD, SAME)
BACK, UNDO = inverse(SPREAD), inverse(REST)


def split3(row):
    high = row.astype(jnp.bfloat16).astype(jnp.float32)
    rest = row - high
    mid = rest.astype(jnp.bfloat16).astype(jnp.float32)
    return [high, mid, rest - mid]


def kernel(
    q_hbm, g_hbm, o_hbm, sums_hbm, k_hbm, v_hbm,
    dq_ref, dk_ref, dv_ref,
    pack, held, blk, part, other, pair, in1, mid, in2, last, k_all, v_all, keys, values, keys_t, acc_k, acc_v,
    kv_sem, held_send, held_recv, blk_send, blk_recv, sib_send, sib_recv, core_send, core_recv,
    one_send, one_recv, two_send, two_recv, last_send, last_recv, out_sem, own_sem, o_own, sums_own,
):
    seq, grp = lax.axis_index("seq"), lax.axis_index("resp")
    z, j = seq // 4, lax.rem(seq, 4)
    xh, core = j // 2, lax.rem(j, 2)
    rows = q_hbm.shape[0]
    positions = dk_ref.shape[0]
    groups = k_all.shape[0] // positions
    scale = q_hbm.shape[1] ** -0.5
    sibling = z * 4 + 2 * xh + (1 - core)

    bits_z = [lax.rem(z, 2), lax.rem(z // 2, 2), z // 4]
    bits_g = [lax.rem(grp, 2), lax.rem(grp // 2, 2), grp // 4]

    def place_of(k):
        return mapped(SPREAD, bits_z, REST, bits_g, ORDER[k])

    def plane_of(k):
        return mapped(joined(BACK, SAME), bits_z, BACK, bits_g, times(BACK, ORDER[k]))

    def head_of(k):
        both = tuple(times(UNDO, c) for c in SPREAD)
        return mapped(both, bits_z, UNDO, bits_g, times(UNDO, ORDER[k]))

    def remote(src, dst, send, recv, seq_to, resp_to):
        return pltpu.make_async_remote_copy(
            src_ref=src, dst_ref=dst, send_sem=send, recv_sem=recv,
            device_id=(seq_to, resp_to), device_id_type=MESH,
        )

    def arrived(ref, sem):
        pltpu.make_async_copy(ref, ref, sem).wait()

    own = [
        pltpu.make_async_copy(src, dst, own_sem.at[i])
        for i, (src, dst) in enumerate((
            (g_hbm, pack.at[rows : 2 * rows]), (o_hbm, o_own), (sums_hbm, sums_own), (q_hbm, pack.at[0:rows]),
        ))
    ]
    for load in own:
        load.start()
    load_k = pltpu.make_async_copy(k_hbm, k_all, kv_sem.at[0])
    load_v = pltpu.make_async_copy(v_hbm, v_all, kv_sem.at[1])
    load_k.start()
    load_v.start()

    barrier = pltpu.get_barrier_semaphore()

    @pl.loop(1, PLANES)
    def _(t):
        pl.semaphore_signal(
            barrier, inc=1, device_id=(lax.rem(z + t, PLANES) * 4 + j, grp), device_id_type=MESH
        )

    @pl.loop(1, 2 * PLANES)
    def _(t):
        peer = lax.rem(grp * 2 + xh + t, 2 * PLANES)
        pl.semaphore_signal(
            barrier, inc=1, device_id=(z * 4 + 2 * lax.rem(peer, 2) + core, peer // 2),
            device_id_type=MESH,
        )

    pl.semaphore_signal(barrier, inc=1, device_id=(sibling, grp), device_id_type=MESH)
    for side in range(2):
        pl.semaphore_signal(
            barrier, inc=1, device_id=(z * 4 + 2 * side + 1 - core, head_of(PLANES - 1)),
            device_id_type=MESH,
        )

    for load in own:
        load.wait()
    product = pack[rows : 2 * rows, :].astype(jnp.float32) * o_own[...].astype(jnp.float32)
    delta = jnp.sum(product.T, axis=0, keepdims=True)
    stats = split3(sums_own[...] * LOG2E) + split3(delta)
    stats = jnp.concatenate(stats + [jnp.zeros((10, rows), jnp.float32)], axis=0)
    pack[2 * rows :, :] = stats.astype(jnp.bfloat16)

    pl.semaphore_wait(barrier, PLANES - 1 + 2 * PLANES - 1 + 1 + 2)

    def move(here, copy, src, dst, recv):
        pl.when(here)(lambda: pltpu.make_async_copy(src, dst, recv).start())
        pl.when(jnp.logical_not(here))(lambda: copy.start())

    def along(k):
        plane = plane_of(k)
        return plane == z, remote(
            pack, held.at[k], held_send.at[k], held_recv.at[k], plane * 4 + j, grp
        )

    def launch(k):
        here, copy = along(k)
        move(here, copy, pack, held.at[k], held_recv.at[k])

    for k in range(WINDOW):
        launch(k)

    def across(k, side):
        head = head_of(k)
        return jnp.logical_and(head == grp, xh == side), remote(
            held.at[k], blk.at[k, core, xh], blk_send.at[k, side], blk_recv.at[k, xh],
            z * 4 + 2 * side + core, head,
        )

    def forward(k):
        arrived(held.at[k], held_recv.at[k])
        for side in range(2):
            here, copy = across(k, side)
            move(here, copy, held.at[k], blk.at[k, core, xh], blk_recv.at[k, xh])

    def to_sibling(k):
        return remote(blk.at[k, core], blk.at[k, core], sib_send.at[k], sib_recv.at[k], sibling, grp)

    def share(k):
        for s in range(2):
            arrived(blk.at[k, core, s], blk_recv.at[k, s])
        to_sibling(k).start()

    load_k.wait()
    load_v.wait()
    tile = 128
    pick = (
        lax.broadcasted_iota(jnp.int32, (tile, tile * groups), 1)
        == lax.broadcasted_iota(jnp.int32, (tile, tile * groups), 0) * groups + grp
    ).astype(jnp.bfloat16)
    for t in range(positions // tile):
        wide, narrow = pl.ds(t * tile * groups, tile * groups), pl.ds(t * tile, tile)
        keys[narrow, :] = lax.dot_general(
            pick, k_all[wide, :], NN, preferred_element_type=jnp.float32
        ).astype(jnp.bfloat16)
        values[narrow, :] = lax.dot_general(
            pick, v_all[wide, :], NN, preferred_element_type=jnp.float32
        ).astype(jnp.bfloat16)
    keys_t[...] = keys[...].T
    acc_k[...] = jnp.zeros_like(acc_k)
    acc_v[...] = jnp.zeros_like(acc_v)

    def work(k):
        parts = [blk.at[k, b // 2, b % 2] for b in range(4)]
        query = jnp.concatenate([p[0:rows, :] for p in parts], axis=0)
        grad = jnp.concatenate([p[rows : 2 * rows, :] for p in parts], axis=0)
        stats = [p[2 * rows :, :].astype(jnp.float32) for p in parts]
        sums = jnp.concatenate([s[0:1] + s[1:2] + s[2:3] for s in stats], axis=1)
        delta = jnp.concatenate([s[3:4] + s[4:5] + s[5:6] for s in stats], axis=1)
        total = None
        for at in range(0, positions, STEP):
            span = pl.ds(at, STEP)
            scores = lax.dot_general(keys[span, :], query, NT, preferred_element_type=jnp.float32)
            probs = lax.dot_general(values[span, :], grad, NT, preferred_element_type=jnp.float32)
            weights = jnp.exp2(scores * (scale * LOG2E) - sums)
            low = weights.astype(jnp.bfloat16)
            grad_scores = (weights * (probs - delta)).astype(jnp.bfloat16)
            acc_v[span, :] += lax.dot_general(low, grad, NN, preferred_element_type=jnp.float32)
            acc_k[span, :] += lax.dot_general(grad_scores, query, NN, preferred_element_type=jnp.float32)
            term = lax.dot_general(keys_t[:, span], grad_scores, NN, preferred_element_type=jnp.float32)
            total = term if total is None else total + term
        total = total.astype(jnp.bfloat16)
        for b in range(4):
            part[k, b // 2, b % 2] = total[:, b * rows : (b + 1) * rows]

    def to_core(k):
        return remote(
            part.at[k, 1 - core], other.at[k], core_send.at[k], core_recv.at[k], sibling, grp
        )

    def spread(k, s):
        place = place_of(k)
        return jnp.logical_and(place == grp, xh == s), remote(
            pair.at[k, s], in1.at[k, xh], one_send.at[k, s], one_recv.at[k, xh],
            z * 4 + 2 * s + core, place,
        )

    def add_cores(k):
        arrived(other.at[k], core_recv.at[k])
        for s in range(2):
            pair[k, s] = (
                part[k, core, s].astype(jnp.float32) + other[k, s].astype(jnp.float32)
            ).astype(jnp.bfloat16)
            here, copy = spread(k, s)
            move(here, copy, pair.at[k, s], in1.at[k, xh], one_recv.at[k, xh])

    def home(k):
        plane = head_of(k)
        return plane == z, remote(
            mid.at[k], in2.at[k], two_send.at[k], two_recv.at[k], plane * 4 + j, grp
        )

    def add_plane(k):
        if k < PLANES - 1:
            terms = [(in1.at[k, s], one_recv.at[k, s]) for s in range(2)]
        else:
            terms = [(last.at[s], last_recv.at[s]) for s in range(4)]
        total = None
        for ref, sem in terms:
            arrived(ref, sem)
            term = ref[...].astype(jnp.float32)
            total = term if total is None else total + term
        mid[k] = total.astype(jnp.bfloat16)
        here, copy = home(k)
        move(here, copy, mid.at[k], in2.at[k], two_recv.at[k])

    def spread_last(b):
        place, owner = place_of(PLANES - 1), (b % 2) * 2 + b // 2
        return jnp.logical_and(place == grp, owner == j), remote(
            part.at[PLANES - 1, b // 2, b % 2], last.at[j], last_send.at[b], last_recv.at[j],
            z * 4 + owner, place,
        )

    def left(here, copy):
        pl.when(jnp.logical_not(here))(lambda: copy.wait_send())

    for k in range(AHEAD):
        forward(k)
    share(0)
    for k in range(PLANES):
        if k + AHEAD < PLANES:
            forward(k + AHEAD)
        if k + 1 < PLANES:
            share(k + 1)
        arrived(blk.at[k, 1 - core], sib_recv.at[k])
        work(k)
        if k < PLANES - 1:
            to_core(k).start()
        else:
            for b in range(4):
                here, copy = spread_last(b)
                move(here, copy, part.at[k, b // 2, b % 2], last.at[j], last_recv.at[j])
        if k >= 1:
            add_cores(k - 1)
        if k >= 4:
            add_plane(k - 4)
    keys[...] = (acc_k[...] * scale).astype(keys.dtype)
    values[...] = acc_v[...].astype(values.dtype)
    outs = [
        pltpu.make_async_copy(keys, dk_ref, out_sem.at[0]),
        pltpu.make_async_copy(values, dv_ref, out_sem.at[1]),
    ]
    for out in outs:
        out.start()
    for k in range(PLANES - 4, PLANES):
        add_plane(k)
    total = jnp.zeros((q_hbm.shape[1], rows), jnp.float32)
    for k in range(PLANES):
        arrived(in2.at[k], two_recv.at[k])
        total += in2[k].astype(jnp.float32)
    dq_ref[...] = (total * scale).T.astype(dq_ref.dtype)

    for k in range(PLANES - WINDOW, PLANES):
        left(*along(k))
    for k in range(PLANES):
        for s in range(2):
            left(*across(k, s))
        to_sibling(k).wait_send()
        left(*home(k))
        if k < PLANES - 1:
            for s in range(2):
                left(*spread(k, s))
            to_core(k).wait_send()
    for b in range(4):
        left(*spread_last(b))
    for out in outs:
        out.wait()


def copy_kernel(*refs):
    half = len(refs) // 2
    for src, dst in zip(refs[:half], refs[half:]):
        dst[...] = src[...]


def per_device(queries, grad_out, outputs, log_sums, prompt_keys, prompt_values):
    rows, dim = queries.shape[2:]
    positions, groups = prompt_keys.shape[:2]
    vmem = pl.BlockSpec(memory_space=pltpu.VMEM)
    hbm = pl.BlockSpec(memory_space=pl.ANY)
    dma = pltpu.SemaphoreType.DMA
    low, full = jnp.bfloat16, jnp.float32
    dq, dk, dv = pl.pallas_call(
        kernel,
        out_shape=(
            jax.ShapeDtypeStruct((rows, dim), low),
            jax.ShapeDtypeStruct((positions, dim), low),
            jax.ShapeDtypeStruct((positions, dim), low),
        ),
        in_specs=[hbm] * 6,
        out_specs=(vmem, hbm, hbm),
        scratch_shapes=[
            pltpu.VMEM((2 * rows + 16, dim), low),
            pltpu.VMEM((PLANES, 2 * rows + 16, dim), low),
            pltpu.VMEM((PLANES, 2, 2, 2 * rows + 16, dim), low),
            pltpu.VMEM((PLANES, 2, 2, dim, rows), low),
            pltpu.VMEM((PLANES, 2, dim, rows), low),
            pltpu.VMEM((PLANES, 2, dim, rows), low),
            pltpu.VMEM((PLANES, 2, dim, rows), low),
            pltpu.VMEM((PLANES, dim, rows), low),
            pltpu.VMEM((PLANES, dim, rows), low),
            pltpu.VMEM((4, dim, rows), low),
            pltpu.VMEM((positions * groups, dim), low),
            pltpu.VMEM((positions * groups, dim), low),
            pltpu.VMEM((positions, dim), low),
            pltpu.VMEM((positions, dim), low),
            pltpu.VMEM((dim, positions), low),
            pltpu.VMEM((positions, dim), full),
            pltpu.VMEM((positions, dim), full),
            dma((2,)), dma((PLANES,)), dma((PLANES,)),
            dma((PLANES, 2)), dma((PLANES, 2)), dma((PLANES,)), dma((PLANES,)),
            dma((PLANES,)), dma((PLANES,)),
            dma((PLANES, 2)), dma((PLANES, 2)), dma((PLANES,)), dma((PLANES,)),
            dma((4,)), dma((4,)), dma((2,)), dma((4,)),
            pltpu.VMEM((rows, dim), low), pltpu.VMEM((1, rows), full),
        ],
        compiler_params=pltpu.CompilerParams(
            collective_id=0, has_side_effects=True, vmem_limit_bytes=60 << 20
        ),
    )(
        queries[0, 0], grad_out[0, 0], outputs[0, 0], log_sums[0],
        prompt_keys.reshape(positions * groups, dim), prompt_values.reshape(positions * groups, dim),
    )
    outs = (dq, dk, dv)
    dq, dk, dv = pl.pallas_call(
        copy_kernel,
        out_shape=tuple(jax.ShapeDtypeStruct(x.shape, x.dtype) for x in outs),
        in_specs=[vmem] * 3,
        out_specs=(vmem,) * 3,
    )(*outs)
    return dq[None, None], dk[:, None, :], dv[:, None, :]


def solution(mesh):
    in_specs = (
        P("resp", "seq", None, None),
        P("resp", "seq", None, None),
        P("resp", "seq", None, None),
        P("resp", "seq", None),
        P("seq", None, None),
        P("seq", None, None),
    )
    out_specs = (P("resp", "seq", None, None), P("seq", "resp", None), P("seq", "resp", None))
    return jax.shard_map(
        per_device, mesh=mesh, in_specs=in_specs, out_specs=out_specs, check_vma=False
    )
```

```python
import functools

import jax
import jax.numpy as jnp
from jax import lax
from jax.experimental import pallas as pl
from jax.experimental.pallas import tpu as pltpu
from jax.sharding import PartitionSpec as P

NT = (((1,), (1,)), ((), ()))
NN = (((1,), (0,)), ((), ()))
MESH = pl.DeviceIdType.MESH
LOG2E = 1.4426950408889634
STEP = 512
PLANES = 8
SPREAD = (4, 3, 6)
ORDER = (2, 5, 0, 4, 7, 3, 1, 6)
AHEAD = 5
WINDOW = 8


def times(columns, value):
    return functools.reduce(lambda x, y: x ^ y, [c for i, c in enumerate(columns) if value >> i & 1], 0)


def inverse(columns):
    return tuple(next(v for v in range(PLANES) if times(columns, v) == 1 << i) for i in range(3))


def mapped(first, a, second, b, constant):
    total = 0
    for i in range(3):
        bit = constant >> i & 1
        for columns, value in ((first, a), (second, b)):
            for n, column in enumerate(columns):
                if column >> i & 1:
                    bit = bit + value[n]
        total = total + lax.rem(bit, 2) * (1 << i)
    return total


def joined(one, two):
    return tuple(x ^ y for x, y in zip(one, two))


SAME = (1, 2, 4)
REST = joined(SPREAD, SAME)
BACK, UNDO = inverse(SPREAD), inverse(REST)


def split3(row):
    high = row.astype(jnp.bfloat16).astype(jnp.float32)
    rest = row - high
    mid = rest.astype(jnp.bfloat16).astype(jnp.float32)
    return [high, mid, rest - mid]


def kernel(
    q_hbm, g_hbm, o_hbm, sums_hbm, k_hbm, v_hbm,
    dq_ref, dk_ref, dv_ref,
    pack, held, blk, part, other, pair, in1, mid, in2, last, k_all, v_all, keys, values, keys_t, acc_k, acc_v,
    kv_sem, held_send, held_recv, blk_send, blk_recv, sib_send, sib_recv, core_send, core_recv,
    one_send, one_recv, two_send, two_recv, last_send, last_recv, out_sem, own_sem, near_send, o_own, sums_own,
):
    seq, grp = lax.axis_index("seq"), lax.axis_index("resp")
    z, j = seq // 4, lax.rem(seq, 4)
    xh, core = j // 2, lax.rem(j, 2)
    rows = q_hbm.shape[0]
    positions = dk_ref.shape[0]
    groups = k_all.shape[0] // positions
    scale = q_hbm.shape[1] ** -0.5
    sibling = z * 4 + 2 * xh + (1 - core)

    bits_z = [lax.rem(z, 2), lax.rem(z // 2, 2), z // 4]
    bits_g = [lax.rem(grp, 2), lax.rem(grp // 2, 2), grp // 4]

    def place_of(k):
        return mapped(SPREAD, bits_z, REST, bits_g, ORDER[k])

    def plane_of(k):
        return mapped(joined(BACK, SAME), bits_z, BACK, bits_g, times(BACK, ORDER[k]))

    def head_of(k):
        both = tuple(times(UNDO, c) for c in SPREAD)
        return mapped(both, bits_z, UNDO, bits_g, times(UNDO, ORDER[k]))

    def remote(src, dst, send, recv, seq_to, resp_to):
        return pltpu.make_async_remote_copy(
            src_ref=src, dst_ref=dst, send_sem=send, recv_sem=recv,
            device_id=(seq_to, resp_to), device_id_type=MESH,
        )

    def arrived(ref, sem):
        pltpu.make_async_copy(ref, ref, sem).wait()

    own = [
        pltpu.make_async_copy(src, dst, own_sem.at[i])
        for i, (src, dst) in enumerate((
            (g_hbm, pack.at[rows : 2 * rows]), (o_hbm, o_own), (sums_hbm, sums_own), (q_hbm, pack.at[0:rows]),
        ))
    ]
    for load in own:
        load.start()
    load_k = pltpu.make_async_copy(k_hbm, k_all, kv_sem.at[0])
    load_v = pltpu.make_async_copy(v_hbm, v_all, kv_sem.at[1])
    load_k.start()
    load_v.start()

    barrier = pltpu.get_barrier_semaphore()

    @pl.loop(1, PLANES)
    def _(t):
        pl.semaphore_signal(
            barrier, inc=1, device_id=(lax.rem(z + t, PLANES) * 4 + j, grp), device_id_type=MESH
        )

    @pl.loop(1, 2 * PLANES)
    def _(t):
        peer = lax.rem(grp * 2 + xh + t, 2 * PLANES)
        pl.semaphore_signal(
            barrier, inc=1, device_id=(z * 4 + 2 * lax.rem(peer, 2) + core, peer // 2),
            device_id_type=MESH,
        )

    pl.semaphore_signal(barrier, inc=1, device_id=(sibling, grp), device_id_type=MESH)
    for side in range(2):
        pl.semaphore_signal(
            barrier, inc=1, device_id=(z * 4 + 2 * side + 1 - core, head_of(PLANES - 1)),
            device_id_type=MESH,
        )

    for load in own:
        load.wait()
    product = pack[rows : 2 * rows, :].astype(jnp.float32) * o_own[...].astype(jnp.float32)
    delta = jnp.sum(product.T, axis=0, keepdims=True)
    stats = split3(sums_own[...] * LOG2E) + split3(delta)
    stats = jnp.concatenate(stats + [jnp.zeros((10, rows), jnp.float32)], axis=0)
    pack[2 * rows :, :] = stats.astype(jnp.bfloat16)

    pl.semaphore_wait(barrier, PLANES - 1 + 2 * PLANES - 1 + 1 + 2)

    def move(here, copy, src, dst, recv):
        pl.when(here)(lambda: pltpu.make_async_copy(src, dst, recv).start())
        pl.when(jnp.logical_not(here))(lambda: copy.start())

    def along(k):
        plane = plane_of(k)
        return plane == z, remote(
            pack, held.at[k], held_send.at[k], held_recv.at[k], plane * 4 + j, grp
        )

    slot = sum(k * (head_of(k) == z).astype(jnp.int32) for k in range(PLANES))

    def near(side):
        return jnp.logical_and(z == grp, xh == side), remote(
            pack, blk.at[slot, core, xh], near_send.at[side], blk_recv.at[slot, xh],
            z * 4 + 2 * side + core, z,
        )

    for side in range(2):
        here, copy = near(side)
        move(here, copy, pack, blk.at[slot, core, xh], blk_recv.at[slot, xh])

    def launch(k):
        here, copy = along(k)
        pl.when(jnp.logical_not(here))(lambda: copy.start())

    for k in range(WINDOW):
        launch(k)

    def across(k, side):
        head = head_of(k)
        return jnp.logical_and(head == grp, xh == side), remote(
            held.at[k], blk.at[k, core, xh], blk_send.at[k, side], blk_recv.at[k, xh],
            z * 4 + 2 * side + core, head,
        )

    def forward(k):
        @pl.when(head_of(k) != z)
        def _():
            arrived(held.at[k], held_recv.at[k])
            for side in range(2):
                here, copy = across(k, side)
                move(here, copy, held.at[k], blk.at[k, core, xh], blk_recv.at[k, xh])

    def to_sibling(k):
        return remote(blk.at[k, core], blk.at[k, core], sib_send.at[k], sib_recv.at[k], sibling, grp)

    def share(k):
        for s in range(2):
            arrived(blk.at[k, core, s], blk_recv.at[k, s])
        to_sibling(k).start()

    load_k.wait()
    load_v.wait()
    tile = 128
    pick = (
        lax.broadcasted_iota(jnp.int32, (tile, tile * groups), 1)
        == lax.broadcasted_iota(jnp.int32, (tile, tile * groups), 0) * groups + grp
    ).astype(jnp.bfloat16)
    for t in range(positions // tile):
        wide, narrow = pl.ds(t * tile * groups, tile * groups), pl.ds(t * tile, tile)
        keys[narrow, :] = lax.dot_general(
            pick, k_all[wide, :], NN, preferred_element_type=jnp.float32
        ).astype(jnp.bfloat16)
        values[narrow, :] = lax.dot_general(
            pick, v_all[wide, :], NN, preferred_element_type=jnp.float32
        ).astype(jnp.bfloat16)
    keys_t[...] = keys[...].T
    acc_k[...] = jnp.zeros_like(acc_k)
    acc_v[...] = jnp.zeros_like(acc_v)

    def work(k):
        parts = [blk.at[k, b // 2, b % 2] for b in range(4)]
        query = jnp.concatenate([p[0:rows, :] for p in parts], axis=0)
        grad = jnp.concatenate([p[rows : 2 * rows, :] for p in parts], axis=0)
        stats = [p[2 * rows :, :].astype(jnp.float32) for p in parts]
        sums = jnp.concatenate([s[0:1] + s[1:2] + s[2:3] for s in stats], axis=1)
        delta = jnp.concatenate([s[3:4] + s[4:5] + s[5:6] for s in stats], axis=1)
        total = None
        for at in range(0, positions, STEP):
            span = pl.ds(at, STEP)
            scores = lax.dot_general(keys[span, :], query, NT, preferred_element_type=jnp.float32)
            probs = lax.dot_general(values[span, :], grad, NT, preferred_element_type=jnp.float32)
            weights = jnp.exp2(scores * (scale * LOG2E) - sums)
            low = weights.astype(jnp.bfloat16)
            grad_scores = (weights * (probs - delta)).astype(jnp.bfloat16)
            acc_v[span, :] += lax.dot_general(low, grad, NN, preferred_element_type=jnp.float32)
            acc_k[span, :] += lax.dot_general(grad_scores, query, NN, preferred_element_type=jnp.float32)
            term = lax.dot_general(keys_t[:, span], grad_scores, NN, preferred_element_type=jnp.float32)
            total = term if total is None else total + term
        total = total.astype(jnp.bfloat16)
        for b in range(4):
            part[k, b // 2, b % 2] = total[:, b * rows : (b + 1) * rows]

    def to_core(k):
        return remote(
            part.at[k, 1 - core], other.at[k], core_send.at[k], core_recv.at[k], sibling, grp
        )

    def spread(k, s):
        place = place_of(k)
        return jnp.logical_and(place == grp, xh == s), remote(
            pair.at[k, s], in1.at[k, xh], one_send.at[k, s], one_recv.at[k, xh],
            z * 4 + 2 * s + core, place,
        )

    def add_cores(k):
        arrived(other.at[k], core_recv.at[k])
        for s in range(2):
            pair[k, s] = (
                part[k, core, s].astype(jnp.float32) + other[k, s].astype(jnp.float32)
            ).astype(jnp.bfloat16)
            here, copy = spread(k, s)
            move(here, copy, pair.at[k, s], in1.at[k, xh], one_recv.at[k, xh])

    def home(k):
        plane = head_of(k)
        return plane == z, remote(
            mid.at[k], in2.at[k], two_send.at[k], two_recv.at[k], plane * 4 + j, grp
        )

    def add_plane(k):
        if k < PLANES - 1:
            terms = [(in1.at[k, s], one_recv.at[k, s]) for s in range(2)]
        else:
            terms = [(last.at[s], last_recv.at[s]) for s in range(4)]
        total = None
        for ref, sem in terms:
            arrived(ref, sem)
            term = ref[...].astype(jnp.float32)
            total = term if total is None else total + term
        mid[k] = total.astype(jnp.bfloat16)
        here, copy = home(k)
        move(here, copy, mid.at[k], in2.at[k], two_recv.at[k])

    def spread_last(b):
        place, owner = place_of(PLANES - 1), (b % 2) * 2 + b // 2
        return jnp.logical_and(place == grp, owner == j), remote(
            part.at[PLANES - 1, b // 2, b % 2], last.at[j], last_send.at[b], last_recv.at[j],
            z * 4 + owner, place,
        )

    def left(here, copy):
        pl.when(jnp.logical_not(here))(lambda: copy.wait_send())

    for k in range(AHEAD):
        forward(k)
    share(0)
    for k in range(PLANES):
        if k + AHEAD < PLANES:
            forward(k + AHEAD)
        if k + 1 < PLANES:
            share(k + 1)
        arrived(blk.at[k, 1 - core], sib_recv.at[k])
        work(k)
        if k < PLANES - 1:
            to_core(k).start()
        else:
            for b in range(4):
                here, copy = spread_last(b)
                move(here, copy, part.at[k, b // 2, b % 2], last.at[j], last_recv.at[j])
        if k >= 1:
            add_cores(k - 1)
        if k >= 4:
            add_plane(k - 4)
    keys[...] = (acc_k[...] * scale).astype(keys.dtype)
    values[...] = acc_v[...].astype(values.dtype)
    outs = [
        pltpu.make_async_copy(keys, dk_ref, out_sem.at[0]),
        pltpu.make_async_copy(values, dv_ref, out_sem.at[1]),
    ]
    for out in outs:
        out.start()
    for k in range(PLANES - 4, PLANES):
        add_plane(k)
    total = jnp.zeros((q_hbm.shape[1], rows), jnp.float32)
    for k in range(PLANES):
        arrived(in2.at[k], two_recv.at[k])
        total += in2[k].astype(jnp.float32)
    dq_ref[...] = (total * scale).T.astype(dq_ref.dtype)

    for k in range(PLANES - WINDOW, PLANES):
        left(*along(k))
    for k in range(PLANES):
        for s in range(2):
            here, copy = across(k, s)
            left(jnp.logical_or(here, head_of(k) == z), copy)
        to_sibling(k).wait_send()
        left(*home(k))
        if k < PLANES - 1:
            for s in range(2):
                left(*spread(k, s))
            to_core(k).wait_send()
    for b in range(4):
        left(*spread_last(b))
    for side in range(2):
        left(*near(side))
    for out in outs:
        out.wait()


def copy_kernel(*refs):
    half = len(refs) // 2
    for src, dst in zip(refs[:half], refs[half:]):
        dst[...] = src[...]


def per_device(queries, grad_out, outputs, log_sums, prompt_keys, prompt_values):
    rows, dim = queries.shape[2:]
    positions, groups = prompt_keys.shape[:2]
    vmem = pl.BlockSpec(memory_space=pltpu.VMEM)
    hbm = pl.BlockSpec(memory_space=pl.ANY)
    dma = pltpu.SemaphoreType.DMA
    low, full = jnp.bfloat16, jnp.float32
    dq, dk, dv = pl.pallas_call(
        kernel,
        out_shape=(
            jax.ShapeDtypeStruct((rows, dim), low),
            jax.ShapeDtypeStruct((positions, dim), low),
            jax.ShapeDtypeStruct((positions, dim), low),
        ),
        in_specs=[hbm] * 6,
        out_specs=(vmem, hbm, hbm),
        scratch_shapes=[
            pltpu.VMEM((2 * rows + 16, dim), low),
            pltpu.VMEM((PLANES, 2 * rows + 16, dim), low),
            pltpu.VMEM((PLANES, 2, 2, 2 * rows + 16, dim), low),
            pltpu.VMEM((PLANES, 2, 2, dim, rows), low),
            pltpu.VMEM((PLANES, 2, dim, rows), low),
            pltpu.VMEM((PLANES, 2, dim, rows), low),
            pltpu.VMEM((PLANES, 2, dim, rows), low),
            pltpu.VMEM((PLANES, dim, rows), low),
            pltpu.VMEM((PLANES, dim, rows), low),
            pltpu.VMEM((4, dim, rows), low),
            pltpu.VMEM((positions * groups, dim), low),
            pltpu.VMEM((positions * groups, dim), low),
            pltpu.VMEM((positions, dim), low),
            pltpu.VMEM((positions, dim), low),
            pltpu.VMEM((dim, positions), low),
            pltpu.VMEM((positions, dim), full),
            pltpu.VMEM((positions, dim), full),
            dma((2,)), dma((PLANES,)), dma((PLANES,)),
            dma((PLANES, 2)), dma((PLANES, 2)), dma((PLANES,)), dma((PLANES,)),
            dma((PLANES,)), dma((PLANES,)),
            dma((PLANES, 2)), dma((PLANES, 2)), dma((PLANES,)), dma((PLANES,)),
            dma((4,)), dma((4,)), dma((2,)), dma((4,)), dma((2,)),
            pltpu.VMEM((rows, dim), low), pltpu.VMEM((1, rows), full),
        ],
        compiler_params=pltpu.CompilerParams(
            collective_id=0, has_side_effects=True, vmem_limit_bytes=60 << 20
        ),
    )(
        queries[0, 0], grad_out[0, 0], outputs[0, 0], log_sums[0],
        prompt_keys.reshape(positions * groups, dim), prompt_values.reshape(positions * groups, dim),
    )
    outs = (dq, dk, dv)
    dq, dk, dv = pl.pallas_call(
        copy_kernel,
        out_shape=tuple(jax.ShapeDtypeStruct(x.shape, x.dtype) for x in outs),
        in_specs=[vmem] * 3,
        out_specs=(vmem,) * 3,
    )(*outs)
    return dq[None, None], dk[:, None, :], dv[:, None, :]


def solution(mesh):
    in_specs = (
        P("resp", "seq", None, None),
        P("resp", "seq", None, None),
        P("resp", "seq", None, None),
        P("resp", "seq", None),
        P("seq", None, None),
        P("seq", None, None),
    )
    out_specs = (P("resp", "seq", None, None), P("seq", "resp", None), P("seq", "resp", None))
    return jax.shard_map(
        per_device, mesh=mesh, in_specs=in_specs, out_specs=out_specs, check_vma=False
    )
```

```python
import functools

import jax
import jax.numpy as jnp
from jax import lax
from jax.experimental import pallas as pl
from jax.experimental.pallas import tpu as pltpu
from jax.sharding import PartitionSpec as P

NT = (((1,), (1,)), ((), ()))
NN = (((1,), (0,)), ((), ()))
MESH = pl.DeviceIdType.MESH
LOG2E = 1.4426950408889634
STEP = 512
PLANES = 8
SPREAD = (4, 3, 6)
ORDER = (2, 5, 0, 4, 7, 3, 1, 6)
AHEAD = 7
WINDOW = 8


def times(columns, value):
    return functools.reduce(lambda x, y: x ^ y, [c for i, c in enumerate(columns) if value >> i & 1], 0)


def inverse(columns):
    return tuple(next(v for v in range(PLANES) if times(columns, v) == 1 << i) for i in range(3))


def mapped(first, a, second, b, constant):
    total = 0
    for i in range(3):
        bit = constant >> i & 1
        for columns, value in ((first, a), (second, b)):
            for n, column in enumerate(columns):
                if column >> i & 1:
                    bit = bit + value[n]
        total = total + lax.rem(bit, 2) * (1 << i)
    return total


def joined(one, two):
    return tuple(x ^ y for x, y in zip(one, two))


SAME = (1, 2, 4)
REST = joined(SPREAD, SAME)
BACK, UNDO = inverse(SPREAD), inverse(REST)


def split3(row):
    high = row.astype(jnp.bfloat16).astype(jnp.float32)
    rest = row - high
    mid = rest.astype(jnp.bfloat16).astype(jnp.float32)
    return [high, mid, rest - mid]


def kernel(
    q_hbm, g_hbm, o_hbm, sums_hbm, k_hbm, v_hbm,
    dq_ref, dk_ref, dv_ref,
    pack, held, blk, part, other, pair, in1, mid, in2, last, k_all, v_all, keys, values, keys_t, acc_k, acc_v,
    kv_sem, held_send, held_recv, blk_send, blk_recv, sib_send, sib_recv, core_send, core_recv,
    one_send, one_recv, two_send, two_recv, last_send, last_recv, out_sem, own_sem, o_own, sums_own,
):
    seq, grp = lax.axis_index("seq"), lax.axis_index("resp")
    z, j = seq // 4, lax.rem(seq, 4)
    xh, core = j // 2, lax.rem(j, 2)
    rows = q_hbm.shape[0]
    positions = dk_ref.shape[0]
    groups = k_all.shape[0] // positions
    scale = q_hbm.shape[1] ** -0.5
    sibling = z * 4 + 2 * xh + (1 - core)

    bits_z = [lax.rem(z, 2), lax.rem(z // 2, 2), z // 4]
    bits_g = [lax.rem(grp, 2), lax.rem(grp // 2, 2), grp // 4]

    def place_of(k):
        return mapped(SPREAD, bits_z, REST, bits_g, ORDER[k])

    def plane_of(k):
        return mapped(joined(BACK, SAME), bits_z, BACK, bits_g, times(BACK, ORDER[k]))

    def head_of(k):
        both = tuple(times(UNDO, c) for c in SPREAD)
        return mapped(both, bits_z, UNDO, bits_g, times(UNDO, ORDER[k]))

    def remote(src, dst, send, recv, seq_to, resp_to):
        return pltpu.make_async_remote_copy(
            src_ref=src, dst_ref=dst, send_sem=send, recv_sem=recv,
            device_id=(seq_to, resp_to), device_id_type=MESH,
        )

    def arrived(ref, sem):
        pltpu.make_async_copy(ref, ref, sem).wait()

    own = [
        pltpu.make_async_copy(src, dst, own_sem.at[i])
        for i, (src, dst) in enumerate((
            (g_hbm, pack.at[rows : 2 * rows]), (o_hbm, o_own), (sums_hbm, sums_own), (q_hbm, pack.at[0:rows]),
        ))
    ]
    for load in own:
        load.start()
    load_k = pltpu.make_async_copy(k_hbm, k_all, kv_sem.at[0])
    load_v = pltpu.make_async_copy(v_hbm, v_all, kv_sem.at[1])
    load_k.start()
    load_v.start()

    barrier = pltpu.get_barrier_semaphore()

    @pl.loop(1, PLANES)
    def _(t):
        pl.semaphore_signal(
            barrier, inc=1, device_id=(lax.rem(z + t, PLANES) * 4 + j, grp), device_id_type=MESH
        )

    @pl.loop(1, 2 * PLANES)
    def _(t):
        peer = lax.rem(grp * 2 + xh + t, 2 * PLANES)
        pl.semaphore_signal(
            barrier, inc=1, device_id=(z * 4 + 2 * lax.rem(peer, 2) + core, peer // 2),
            device_id_type=MESH,
        )

    pl.semaphore_signal(barrier, inc=1, device_id=(sibling, grp), device_id_type=MESH)
    for side in range(2):
        pl.semaphore_signal(
            barrier, inc=1, device_id=(z * 4 + 2 * side + 1 - core, head_of(PLANES - 1)),
            device_id_type=MESH,
        )

    for load in own:
        load.wait()
    product = pack[rows : 2 * rows, :].astype(jnp.float32) * o_own[...].astype(jnp.float32)
    delta = jnp.sum(product.T, axis=0, keepdims=True)
    stats = split3(sums_own[...] * LOG2E) + split3(delta)
    stats = jnp.concatenate(stats + [jnp.zeros((10, rows), jnp.float32)], axis=0)
    pack[2 * rows :, :] = stats.astype(jnp.bfloat16)

    pl.semaphore_wait(barrier, PLANES - 1 + 2 * PLANES - 1 + 1 + 2)

    def move(here, copy, src, dst, recv):
        pl.when(here)(lambda: pltpu.make_async_copy(src, dst, recv).start())
        pl.when(jnp.logical_not(here))(lambda: copy.start())

    def along(k):
        plane = plane_of(k)
        return plane == z, remote(
            pack, held.at[k], held_send.at[k], held_recv.at[k], plane * 4 + j, grp
        )

    def launch(k):
        here, copy = along(k)
        move(here, copy, pack, held.at[k], held_recv.at[k])

    for k in range(WINDOW):
        launch(k)

    def across(k, side):
        head = head_of(k)
        return jnp.logical_and(head == grp, xh == side), remote(
            held.at[k], blk.at[k, core, xh], blk_send.at[k, side], blk_recv.at[k, xh],
            z * 4 + 2 * side + core, head,
        )

    def forward(k):
        arrived(held.at[k], held_recv.at[k])
        for side in range(2):
            here, copy = across(k, side)
            move(here, copy, held.at[k], blk.at[k, core, xh], blk_recv.at[k, xh])

    def to_sibling(k):
        return remote(blk.at[k, core], blk.at[k, core], sib_send.at[k], sib_recv.at[k], sibling, grp)

    def share(k):
        for s in range(2):
            arrived(blk.at[k, core, s], blk_recv.at[k, s])
        to_sibling(k).start()

    load_k.wait()
    load_v.wait()
    tile = 128
    pick = (
        lax.broadcasted_iota(jnp.int32, (tile, tile * groups), 1)
        == lax.broadcasted_iota(jnp.int32, (tile, tile * groups), 0) * groups + grp
    ).astype(jnp.bfloat16)
    for t in range(positions // tile):
        wide, narrow = pl.ds(t * tile * groups, tile * groups), pl.ds(t * tile, tile)
        keys[narrow, :] = lax.dot_general(
            pick, k_all[wide, :], NN, preferred_element_type=jnp.float32
        ).astype(jnp.bfloat16)
        values[narrow, :] = lax.dot_general(
            pick, v_all[wide, :], NN, preferred_element_type=jnp.float32
        ).astype(jnp.bfloat16)
    keys_t[...] = keys[...].T
    acc_k[...] = jnp.zeros_like(acc_k)
    acc_v[...] = jnp.zeros_like(acc_v)

    def work(k):
        parts = [blk.at[k, b // 2, b % 2] for b in range(4)]
        query = jnp.concatenate([p[0:rows, :] for p in parts], axis=0)
        grad = jnp.concatenate([p[rows : 2 * rows, :] for p in parts], axis=0)
        stats = [p[2 * rows :, :].astype(jnp.float32) for p in parts]
        sums = jnp.concatenate([s[0:1] + s[1:2] + s[2:3] for s in stats], axis=1)
        delta = jnp.concatenate([s[3:4] + s[4:5] + s[5:6] for s in stats], axis=1)
        total = None
        for at in range(0, positions, STEP):
            span = pl.ds(at, STEP)
            scores = lax.dot_general(keys[span, :], query, NT, preferred_element_type=jnp.float32)
            probs = lax.dot_general(values[span, :], grad, NT, preferred_element_type=jnp.float32)
            weights = jnp.exp2(scores * (scale * LOG2E) - sums)
            low = weights.astype(jnp.bfloat16)
            grad_scores = (weights * (probs - delta)).astype(jnp.bfloat16)
            acc_v[span, :] += lax.dot_general(low, grad, NN, preferred_element_type=jnp.float32)
            acc_k[span, :] += lax.dot_general(grad_scores, query, NN, preferred_element_type=jnp.float32)
            term = lax.dot_general(keys_t[:, span], grad_scores, NN, preferred_element_type=jnp.float32)
            total = term if total is None else total + term
        total = total.astype(jnp.bfloat16)
        for b in range(4):
            part[k, b // 2, b % 2] = total[:, b * rows : (b + 1) * rows]

    def to_core(k):
        return remote(
            part.at[k, 1 - core], other.at[k], core_send.at[k], core_recv.at[k], sibling, grp
        )

    def spread(k, s):
        place = place_of(k)
        return jnp.logical_and(place == grp, xh == s), remote(
            pair.at[k, s], in1.at[k, xh], one_send.at[k, s], one_recv.at[k, xh],
            z * 4 + 2 * s + core, place,
        )

    def add_cores(k):
        arrived(other.at[k], core_recv.at[k])
        for s in range(2):
            pair[k, s] = (
                part[k, core, s].astype(jnp.float32) + other[k, s].astype(jnp.float32)
            ).astype(jnp.bfloat16)
            here, copy = spread(k, s)
            move(here, copy, pair.at[k, s], in1.at[k, xh], one_recv.at[k, xh])

    def home(k):
        plane = head_of(k)
        return plane == z, remote(
            mid.at[k], in2.at[k], two_send.at[k], two_recv.at[k], plane * 4 + j, grp
        )

    def add_plane(k):
        if k < PLANES - 1:
            terms = [(in1.at[k, s], one_recv.at[k, s]) for s in range(2)]
        else:
            terms = [(last.at[s], last_recv.at[s]) for s in range(4)]
        total = None
        for ref, sem in terms:
            arrived(ref, sem)
            term = ref[...].astype(jnp.float32)
            total = term if total is None else total + term
        mid[k] = total.astype(jnp.bfloat16)
        here, copy = home(k)
        move(here, copy, mid.at[k], in2.at[k], two_recv.at[k])

    def spread_last(b):
        place, owner = place_of(PLANES - 1), (b % 2) * 2 + b // 2
        return jnp.logical_and(place == grp, owner == j), remote(
            part.at[PLANES - 1, b // 2, b % 2], last.at[j], last_send.at[b], last_recv.at[j],
            z * 4 + owner, place,
        )

    def left(here, copy):
        pl.when(jnp.logical_not(here))(lambda: copy.wait_send())

    for k in range(AHEAD):
        forward(k)
    share(0)
    for k in range(PLANES):
        if k + AHEAD < PLANES:
            forward(k + AHEAD)
        if k + 1 < PLANES:
            share(k + 1)
        arrived(blk.at[k, 1 - core], sib_recv.at[k])
        work(k)
        if k < PLANES - 1:
            to_core(k).start()
        else:
            for b in range(4):
                here, copy = spread_last(b)
                move(here, copy, part.at[k, b // 2, b % 2], last.at[j], last_recv.at[j])
        if k >= 1:
            add_cores(k - 1)
        if k >= 4:
            add_plane(k - 4)
    keys[...] = (acc_k[...] * scale).astype(keys.dtype)
    values[...] = acc_v[...].astype(values.dtype)
    outs = [
        pltpu.make_async_copy(keys, dk_ref, out_sem.at[0]),
        pltpu.make_async_copy(values, dv_ref, out_sem.at[1]),
    ]
    for out in outs:
        out.start()
    for k in range(PLANES - 4, PLANES):
        add_plane(k)
    total = jnp.zeros((q_hbm.shape[1], rows), jnp.float32)
    for k in range(PLANES):
        arrived(in2.at[k], two_recv.at[k])
        total += in2[k].astype(jnp.float32)
    dq_ref[...] = (total * scale).T.astype(dq_ref.dtype)

    for k in range(PLANES - WINDOW, PLANES):
        left(*along(k))
    for k in range(PLANES):
        for s in range(2):
            left(*across(k, s))
        to_sibling(k).wait_send()
        left(*home(k))
        if k < PLANES - 1:
            for s in range(2):
                left(*spread(k, s))
            to_core(k).wait_send()
    for b in range(4):
        left(*spread_last(b))
    for out in outs:
        out.wait()


def copy_kernel(*refs):
    half = len(refs) // 2
    for src, dst in zip(refs[:half], refs[half:]):
        dst[...] = src[...]


def per_device(queries, grad_out, outputs, log_sums, prompt_keys, prompt_values):
    rows, dim = queries.shape[2:]
    positions, groups = prompt_keys.shape[:2]
    vmem = pl.BlockSpec(memory_space=pltpu.VMEM)
    hbm = pl.BlockSpec(memory_space=pl.ANY)
    dma = pltpu.SemaphoreType.DMA
    low, full = jnp.bfloat16, jnp.float32
    dq, dk, dv = pl.pallas_call(
        kernel,
        out_shape=(
            jax.ShapeDtypeStruct((rows, dim), low),
            jax.ShapeDtypeStruct((positions, dim), low),
            jax.ShapeDtypeStruct((positions, dim), low),
        ),
        in_specs=[hbm] * 6,
        out_specs=(vmem, hbm, hbm),
        scratch_shapes=[
            pltpu.VMEM((2 * rows + 16, dim), low),
            pltpu.VMEM((PLANES, 2 * rows + 16, dim), low),
            pltpu.VMEM((PLANES, 2, 2, 2 * rows + 16, dim), low),
            pltpu.VMEM((PLANES, 2, 2, dim, rows), low),
            pltpu.VMEM((PLANES, 2, dim, rows), low),
            pltpu.VMEM((PLANES, 2, dim, rows), low),
            pltpu.VMEM((PLANES, 2, dim, rows), low),
            pltpu.VMEM((PLANES, dim, rows), low),
            pltpu.VMEM((PLANES, dim, rows), low),
            pltpu.VMEM((4, dim, rows), low),
            pltpu.VMEM((positions * groups, dim), low),
            pltpu.VMEM((positions * groups, dim), low),
            pltpu.VMEM((positions, dim), low),
            pltpu.VMEM((positions, dim), low),
            pltpu.VMEM((dim, positions), low),
            pltpu.VMEM((positions, dim), full),
            pltpu.VMEM((positions, dim), full),
            dma((2,)), dma((PLANES,)), dma((PLANES,)),
            dma((PLANES, 2)), dma((PLANES, 2)), dma((PLANES,)), dma((PLANES,)),
            dma((PLANES,)), dma((PLANES,)),
            dma((PLANES, 2)), dma((PLANES, 2)), dma((PLANES,)), dma((PLANES,)),
            dma((4,)), dma((4,)), dma((2,)), dma((4,)),
            pltpu.VMEM((rows, dim), low), pltpu.VMEM((1, rows), full),
        ],
        compiler_params=pltpu.CompilerParams(
            collective_id=0, has_side_effects=True, vmem_limit_bytes=60 << 20
        ),
    )(
        queries[0, 0], grad_out[0, 0], outputs[0, 0], log_sums[0],
        prompt_keys.reshape(positions * groups, dim), prompt_values.reshape(positions * groups, dim),
    )
    outs = (dq, dk, dv)
    dq, dk, dv = pl.pallas_call(
        copy_kernel,
        out_shape=tuple(jax.ShapeDtypeStruct(x.shape, x.dtype) for x in outs),
        in_specs=[vmem] * 3,
        out_specs=(vmem,) * 3,
    )(*outs)
    return dq[None, None], dk[:, None, :], dv[:, None, :]


def solution(mesh):
    in_specs = (
        P("resp", "seq", None, None),
        P("resp", "seq", None, None),
        P("resp", "seq", None, None),
        P("resp", "seq", None),
        P("seq", None, None),
        P("seq", None, None),
    )
    out_specs = (P("resp", "seq", None, None), P("seq", "resp", None), P("seq", "resp", None))
    return jax.shard_map(
        per_device, mesh=mesh, in_specs=in_specs, out_specs=out_specs, check_vma=False
    )
```
